32 devices in a mesh: shard: 4 (over y, x), node: 4 (over z), replica: 2 (over core).
Axes of the slice: x: 2, y: 2, z: 4, core: 2. Of those that a mesh axis runs over, the one named last changes fastest.
Arguments:
- tokens: bfloat16 [6144, 8192], P(('shard', 'node', 'replica')), may hold values from -6 to 6
- weight_codes: bfloat16 [8192, 256], P('shard'), may hold values from -4 to 4
- scale_powers: int32 [64, 256], replicated, may hold values from 5 to 8
- cotangent: bfloat16 [6144, 256], P(('shard', 'node', 'replica')), may hold values from -0.078125 to 0.078125
Outputs:
- keys_values: bfloat16 [6144, 256], P(('shard', 'node', 'replica'))
- weight_grad: float32 [8192, 256], P(('shard', 'node', 'replica'))
The draws below stay inside these ranges and needn't reach their ends.
All inputs are finite; a program needn't handle non-finite values.
Results may differ from the reference program's by a relative error of at most 0.0028.
Values may be sent and summed in bfloat16 or wider, within the bound.
A program may use at most 64 MiB of HBM per device.

```python
import jax
import jax.numpy as jnp
from jax import lax

D = 8192
HD = 128
BLOCK = 128
TOK_DEV = 192
TOKENS = 6144
DEVICES = 32


def with_ends(array, key, least, high):
    spot = [jax.random.randint(jax.random.fold_in(key, axis), (), 0, length) for axis, length in enumerate(array.shape)]
    main_axis = array.shape.index(max(array.shape))
    beside = spot[:main_axis] + [(spot[main_axis] + 1) % array.shape[main_axis]] + spot[main_axis + 1:]
    return array.at[tuple(spot)].set(least).at[tuple(beside)].set(high)


def spiked(array, own_key, source, target, parts, factor):
    owner, partner = [(jnp.arange(array.shape[dim]) // (array.shape[dim] // parts)).reshape([-1 if axis == dim else 1 for axis in range(array.ndim)]) for dim in (source, target)]
    chosen = jax.random.permutation(own_key, parts)[partner]
    strong = (owner == chosen) | (owner == (partner + parts // 2) % parts)
    return jnp.where(strong, factor * array, array)


def steps_of(key, extent, cuts, low, top_value):
    loudness, own = 1.0, jax.random.fold_in(key, 6)
    for axis_at, blocks in cuts:
        heights = jnp.exp(jax.random.uniform(jax.random.fold_in(own, axis_at), (blocks,), jnp.float32, low / len(cuts), top_value / len(cuts)))
        loudness = loudness * jnp.repeat(heights, extent[axis_at] // blocks).reshape([-1 if axis == axis_at else 1 for axis in range(len(extent))])
    return loudness


def bell_draw(stream_key, extent, spread, limit, cuts=(), dtype=jnp.bfloat16):
    values = jax.random.normal(stream_key, extent, jnp.float32) * spread
    if len(cuts) > 0:
        values = steps_of(stream_key, extent, cuts, -0.22, 0.18) * values
    return jnp.clip(values, min=-limit, max=limit).astype(dtype)


def noise_with(own_key, dims, deviation, limit, pieces, heavy, dtype=jnp.bfloat16):
    entries = deviation * jax.random.normal(own_key, dims, jnp.float32)
    if pieces:
        entries = entries * steps_of(own_key, dims, pieces, -0.22, 0.18)
    return jnp.clip(spiked(entries, jax.random.fold_in(own_key, 3), *heavy), -limit, limit).astype(dtype)


def setup_inputs(seed: int = 0) -> dict:
    splits = jax.random.split(jax.random.key(seed), 5)
    tokens = noise_with(splits[0], (TOKENS, D), 1.0, 6.0, ((0, 32),), (0, 1, 32, 2.75))
    weight_codes = bell_draw(splits[1], (D, 2 * HD), 1.0, 4.0, ((0, 4),))
    scale_powers = with_ends(jax.random.randint(splits[2], (D // BLOCK, 2 * HD), 5, 9), jax.random.fold_in(splits[2], 1), 5, 8).astype(jnp.int32)
    cotangent = bell_draw(splits[3], (TOKENS, 2 * HD), TOKENS ** -0.5, 0.078125, ((0, 32),))
    return dict(tokens=tokens, weight_codes=weight_codes, scale_powers=scale_powers, cotangent=cotangent)


def reference(tokens, weight_codes, scale_powers, cotangent):
    factors = jnp.repeat(jnp.exp2(-scale_powers.astype(jnp.float32)), BLOCK, axis=0)
    weight = (weight_codes.astype(jnp.float32) * factors).astype(jnp.bfloat16)
    keys_values = jnp.dot(tokens, weight, preferred_element_type=jnp.float32).astype(jnp.bfloat16)
    token_blocks = tokens.reshape(DEVICES, TOK_DEV, D)
    grad_blocks = cotangent.reshape(DEVICES, TOK_DEV, 2 * HD)

    def accumulate(total, pair):
        block_tokens, block_grads = pair
        partial_value = lax.dot_general(block_tokens, block_grads, (((0,), (0,)), ((), ())), preferred_element_type=jnp.float32)
        return total + partial_value, None

    start_total = jnp.zeros((D, 2 * HD), jnp.float32)
    weight_grad, unused = lax.scan(accumulate, start_total, (token_blocks, grad_blocks))
    return keys_values, weight_grad
```

```python
import functools

import jax
import jax.numpy as jnp
from jax import lax
from jax.experimental import pallas as pl
from jax.experimental.pallas import tpu as pltpu
from jax.sharding import PartitionSpec as P

BLOCK = 128
MESH = pl.DeviceIdType.MESH
OFF = (2, 1, 3, 0)
D_, X_, Y_, O_ = 0, 1, 2, 3
F32, BF16 = jnp.float32, jnp.bfloat16


def generic(tokens, weight_codes, scale_powers, cotangent):
    factors = jnp.repeat(jnp.exp2(-scale_powers.astype(jnp.float32)), BLOCK, axis=0)
    codes = lax.all_gather(weight_codes, "shard", axis=0, tiled=True)
    weight = (codes.astype(jnp.float32) * factors).astype(jnp.bfloat16)
    projected = jnp.dot(tokens, weight, preferred_element_type=jnp.float32)
    keys_values = projected.astype(jnp.bfloat16)
    partial_value = lax.dot_general(
        tokens, cotangent, (((0,), (0,)), ((), ())), preferred_element_type=jnp.float32
    )
    inner = lax.psum_scatter(partial_value, "shard", scatter_dimension=0, tiled=True)
    weight_grad = lax.psum_scatter(inner, ("node", "replica"), scatter_dimension=0, tiled=True)
    return (keys_values, weight_grad)


def kernel(tokens, codes, scales, cot, kv_out, wg_out,
           tokv, tokk, cot2, cott, wown, wbuf, s1x, s1y, r1x, r1y,
           s2x, s2y, r2x, r2y, gown, gx, gy, zs, zr, acc, ls, ss, rs):
    s, n, r = lax.axis_index("shard"), lax.axis_index("node"), lax.axis_index("replica")
    xs = s + 1 - 2 * lax.rem(s, 2)
    ys = s + 2 - 4 * lax.div(s, 2)
    dest = (3 - s, xs, ys, s)
    nodes = [lax.rem(n + off, 4) for off in OFF]
    sib, to_x, to_y = {"replica": 1 - r}, {"shard": xs}, {"shard": ys}
    to_z = [{"node": nodes[j]} for j in range(3)]
    T = cot.shape[0]

    nl = [0]
    sent = []

    def local(src, dst):
        c = pltpu.make_async_copy(src, dst, ls.at[nl[0]])
        nl[0] += 1
        c.start()
        return c

    def remote(src, dst, device):
        i = len(sent)
        c = pltpu.make_async_remote_copy(
            src_ref=src, dst_ref=dst, send_sem=ss.at[i], recv_sem=rs.at[i],
            device_id=device, device_id_type=MESH)
        sent.append(c)
        c.start()
        return c

    def columns(d, k, which):
        return pl.ds(pl.multiple_of(((dest[d] * 4 + nodes[k]) * 2 + which) * 256, 256), 256)

    barrier = pltpu.get_barrier_semaphore()
    for peer in [sib, to_x, to_y] + to_z:
        pl.semaphore_signal(barrier, inc=1, device_id=peer, device_id_type=MESH)

    own_tok = {}
    for k in range(4):
        for d in (D_, X_, Y_, O_):
            own_tok[d, k] = local(tokens.at[:, columns(d, k, r)], tokk.at[k * 4 + d, pl.ds(0, T)])
    load_w = local(codes, wown)
    load_tok = [None] * 4
    for d in (O_, X_, Y_, D_):
        load_tok[d] = local(
            tokens.at[:, pl.ds(pl.multiple_of(dest[d] * 2048, 2048), 2048)], tokv.at[d])
    cot2[pl.ds(0, T)] = cot[...]

    pl.semaphore_wait(barrier, 6)

    cot_c = remote(cot, cot2.at[pl.ds(T, T)], sib)
    sib_tok = {}

    def send_tok(d, k):
        sib_tok[d, k] = remote(
            tokens.at[:, columns(d, k, 1 - r)], tokk.at[k * 4 + d, pl.ds(T, T)], sib)

    for d in (D_, X_, Y_):
        send_tok(d, 0)

    def quarter(q):
        return pl.ds(pl.multiple_of((2 * r + q) * 512, 512), 512)

    ag = {}
    ag[X_, 0] = remote(codes.at[quarter(0)], wbuf.at[0, 2 * r + 0], to_x)
    ag[Y_, 1] = remote(codes.at[quarter(1)], wbuf.at[1, 2 * r + 1], to_y)
    for k in range(1, 4):
        for d in (D_, X_, Y_):
            send_tok(d, k)
    for k in range(4):
        send_tok(O_, k)
    ag[X_, 1] = remote(codes.at[quarter(1)], wbuf.at[0, 2 * r + 1], to_x)
    ag[Y_, 0] = remote(codes.at[quarter(0)], wbuf.at[1, 2 * r + 0], to_y)

    cot_c.wait_recv()
    cott[...] = cot2[...].astype(F32).T.astype(BF16)

    def grad(d, k):
        own_tok[d, k].wait()
        sib_tok[d, k].wait_recv()
        return jnp.dot(cott[...], tokk[k * 4 + d], preferred_element_type=F32)

    step1x, step1y, step2x, step2y, zc = {}, {}, {}, {}, {}
    for k in range(4):
        g = grad(D_, k)
        s1x[k, 1] = g[:128].astype(BF16)
        s1y[k, 1] = g[128:].astype(BF16)
        g = grad(X_, k)
        s1x[k, 0] = g[:128].astype(BF16)
        gx[k] = g[128:]
        step1x[k] = remote(s1x.at[k], r1x.at[k], to_x)
        g = grad(Y_, k)
        s1y[k, 0] = g[128:].astype(BF16)
        gy[k] = g[:128]
        step1y[k] = remote(s1y.at[k], r1y.at[k], to_y)

    sw = {}

    def to_sib(d, q):
        slot = {X_: 0, Y_: 1, D_: 2}[d]
        sw[d, q] = remote(wbuf.at[slot, 2 * r + q], wbuf.at[slot, 2 * r + q], sib)

    ag[X_, 0].wait_recv()
    ag[D_, 0] = remote(wbuf.at[0, 2 * r + 0], wbuf.at[2, 2 * r + 0], to_y)
    to_sib(X_, 0)
    ag[Y_, 1].wait_recv()
    ag[D_, 1] = remote(wbuf.at[1, 2 * r + 1], wbuf.at[2, 2 * r + 1], to_x)
    to_sib(Y_, 1)

    for k in range(4):
        gown[k] = grad(O_, k)

    def project(d, load):
        load_tok[d].wait()
        p = scales[pl.ds(pl.multiple_of(dest[d] * 16, 16), 16), :]
        fac = jnp.where(p == 5, 2.0 ** -5, jnp.where(p == 6, 2.0 ** -6, jnp.where(p == 7, 2.0 ** -7, 2.0 ** -8))).astype(F32)
        total = None
        for c in range(4):
            w = load(c).astype(F32)
            w = jnp.concatenate(
                [w[b * 128:(b + 1) * 128] * fac[c * 4 + b:c * 4 + b + 1, :] for b in range(4)], axis=0
            ).astype(BF16)
            part = jnp.dot(tokv[d, :, c * 512:(c + 1) * 512], w, preferred_element_type=F32)
            total = part if total is None else total + part
        return total

    load_w.wait()
    acc[...] = project(O_, lambda c: wown[c * 512:(c + 1) * 512])

    def second(k):
        step1x[k].wait_recv()
        s2y[k] = (gy[k] + r1x[k, 1].astype(F32)).astype(BF16)
        step2y[k] = remote(s2y.at[k], r2y.at[k], to_y)
        step1y[k].wait_recv()
        s2x[k] = (gx[k] + r1y[k, 1].astype(F32)).astype(BF16)
        step2x[k] = remote(s2x.at[k], r2x.at[k], to_x)

    def plane(k):
        step2y[k].wait_recv()
        top = gown[k, :128] + r1x[k, 0].astype(F32) + r2y[k].astype(F32)
        step2x[k].wait_recv()
        bottom = gown[k, 128:] + r1y[k, 0].astype(F32) + r2x[k].astype(F32)
        if k < 3:
            zs[k, :128] = top.astype(BF16)
            zs[k, 128:] = bottom.astype(BF16)
            zc[k] = remote(zs.at[k], zr.at[k], to_z[k])
        else:
            gown[k, :128] = top
            gown[k, 128:] = bottom

    def pass_on(d, q):
        ag[d, q].wait_recv()
        to_sib(d, q)

    def arrive(d):
        sw[d, 0].wait_recv()
        sw[d, 1].wait_recv()

    second(0)
    pass_on(X_, 1)
    pass_on(Y_, 0)
    second(1)
    plane(0)
    arrive(X_)
    acc[...] += project(X_, lambda c: wbuf[0, c])
    second(2)
    plane(1)
    arrive(Y_)
    acc[...] += project(Y_, lambda c: wbuf[1, c])
    second(3)
    plane(2)
    pass_on(D_, 0)
    pass_on(D_, 1)
    plane(3)
    arrive(D_)
    kv_out[...] = (acc[...] + project(D_, lambda c: wbuf[2, c])).astype(BF16)
    total = gown[3]
    for k in range(3):
        zc[k].wait_recv()
        total = total + zr[k].astype(F32)
    wg_out[...] = total.T
    for c in sent:
        c.wait_send()


def special(tokens, weight_codes, scale_powers, cotangent):
    T = tokens.shape[0]
    vm = pltpu.VMEM
    n_local, n_remote = 16 + 1 + 4, 49
    return tuple(pl.pallas_call(
        kernel,
        out_shape=(jax.ShapeDtypeStruct((T, 256), BF16), jax.ShapeDtypeStruct((256, 256), F32)),
        in_specs=[
            pl.BlockSpec(memory_space=pl.ANY), pl.BlockSpec(memory_space=pl.ANY),
            pl.BlockSpec(memory_space=vm), pl.BlockSpec(memory_space=vm)],
        out_specs=(pl.BlockSpec(memory_space=vm), pl.BlockSpec(memory_space=vm)),
        scratch_shapes=[
            vm((4, T, 2048), BF16), vm((16, 2 * T, 256), BF16), vm((2 * T, 256), BF16), vm((256, 2 * T), BF16),
            vm((2048, 256), BF16), vm((3, 4, 512, 256), BF16),
            vm((4, 2, 128, 256), BF16), vm((4, 2, 128, 256), BF16),
            vm((4, 2, 128, 256), BF16), vm((4, 2, 128, 256), BF16),
            vm((4, 128, 256), BF16), vm((4, 128, 256), BF16),
            vm((4, 128, 256), BF16), vm((4, 128, 256), BF16),
            vm((4, 256, 256), F32), vm((4, 128, 256), F32), vm((4, 128, 256), F32),
            vm((3, 256, 256), BF16), vm((3, 256, 256), BF16), vm((T, 256), F32),
            pltpu.SemaphoreType.DMA((n_local,)),
            pltpu.SemaphoreType.DMA((n_remote,)),
            pltpu.SemaphoreType.DMA((n_remote,)),
        ],
        compiler_params=pltpu.CompilerParams(
            collective_id=0, has_side_effects=True, vmem_limit_bytes=40 * 1024 * 1024),
        cost_estimate=pl.CostEstimate(flops=1_700_000_000, bytes_accessed=6_000_000, transcendentals=0),
    )(tokens, weight_codes, scale_powers, cotangent))


def solution(mesh):
    placed = (
        P(("shard", "node", "replica"), None),
        P("shard", None),
        P(),
        P(("shard", "node", "replica"), None),
    )
    small = tuple(mesh.shape[a] for a in ("shard", "node", "replica")) == (4, 4, 2)
    return jax.shard_map(
        special if small else generic,
        mesh=mesh,
        in_specs=placed,
        out_specs=(P(("shard", "node", "replica"), None), P(("shard", "node", "replica"), None)),
        check_vma=False,
    )
```

```python
import functools

import jax
import jax.numpy as jnp
from jax import lax
from jax.experimental import pallas as pl
from jax.experimental.pallas import tpu as pltpu
from jax.sharding import PartitionSpec as P

BLOCK = 128
MESH = pl.DeviceIdType.MESH
OFF = (2, 1, 3, 0)
D_, X_, Y_, O_ = 0, 1, 2, 3
F32, BF16 = jnp.float32, jnp.bfloat16


def generic(tokens, weight_codes, scale_powers, cotangent):
    factors = jnp.repeat(jnp.exp2(-scale_powers.astype(jnp.float32)), BLOCK, axis=0)
    codes = lax.all_gather(weight_codes, "shard", axis=0, tiled=True)
    weight = (codes.astype(jnp.float32) * factors).astype(jnp.bfloat16)
    projected = jnp.dot(tokens, weight, preferred_element_type=jnp.float32)
    keys_values = projected.astype(jnp.bfloat16)
    partial_value = lax.dot_general(
        tokens, cotangent, (((0,), (0,)), ((), ())), preferred_element_type=jnp.float32
    )
    inner = lax.psum_scatter(partial_value, "shard", scatter_dimension=0, tiled=True)
    weight_grad = lax.psum_scatter(inner, ("node", "replica"), scatter_dimension=0, tiled=True)
    return (keys_values, weight_grad)


def kernel(tokens, codes, scales_in, cot, kv_out, wg_out,
           tokv, tokk, cot2, cott, wown, wbuf, s1x, s1y, r1x, r1y,
           s2x, s2y, r2x, r2y, gown, gx, gy, zs, zr, acc, scales, ls, ss, rs):
    s, n, r = lax.axis_index("shard"), lax.axis_index("node"), lax.axis_index("replica")
    xs = s + 1 - 2 * lax.rem(s, 2)
    ys = s + 2 - 4 * lax.div(s, 2)
    dest = (3 - s, xs, ys, s)
    nodes = [lax.rem(n + off, 4) for off in OFF]
    sib, to_x, to_y = {"replica": 1 - r}, {"shard": xs}, {"shard": ys}
    to_z = [{"node": nodes[j]} for j in range(3)]
    T = cot.shape[0]
    par = lax.rem(n, 2)
    mine, theirs = 2 * r + par, 2 * r + 1 - par
    to_pair = {"node": n + 1 - 2 * par}

    nl = [0]
    sent = []

    def local(src, dst):
        c = pltpu.make_async_copy(src, dst, ls.at[nl[0]])
        nl[0] += 1
        c.start()
        return c

    def remote(src, dst, device):
        i = len(sent)
        c = pltpu.make_async_remote_copy(
            src_ref=src, dst_ref=dst, send_sem=ss.at[i], recv_sem=rs.at[i],
            device_id=device, device_id_type=MESH)
        sent.append(c)
        c.start()
        return c

    def columns(d, k, which):
        return pl.ds(pl.multiple_of(((dest[d] * 4 + nodes[k]) * 2 + which) * 256, 256), 256)

    barrier = pltpu.get_barrier_semaphore()
    for peer in [sib, to_x, to_y] + to_z:
        pl.semaphore_signal(barrier, inc=1, device_id=peer, device_id_type=MESH)

    load_cot = local(cot, cot2.at[pl.ds(0, T)])
    load_sc = local(scales_in, scales)
    own_tok = {}
    for k in range(4):
        for d in (D_, X_, Y_, O_):
            own_tok[d, k] = local(tokens.at[:, columns(d, k, r)], tokk.at[k * 4 + d, pl.ds(0, T)])
    load_w = local(codes, wown)
    load_tok = [None] * 4
    for d in (O_, X_, Y_, D_):
        load_tok[d] = local(
            tokens.at[:, pl.ds(pl.multiple_of(dest[d] * 2048, 2048), 2048)], tokv.at[d])

    pl.semaphore_wait(barrier, 6)

    cot_c = remote(cot, cot2.at[pl.ds(T, T)], sib)
    sib_tok = {}

    def send_tok(d, k):
        sib_tok[d, k] = remote(
            tokens.at[:, columns(d, k, 1 - r)], tokk.at[k * 4 + d, pl.ds(T, T)], sib)

    for d in (D_, X_, Y_):
        send_tok(d, 0)

    rows = pl.ds(pl.multiple_of(mine * 512, 512), 512)
    ag = {}
    ag[X_] = remote(codes.at[rows], wbuf.at[0, mine], to_x)
    ag[Y_] = remote(codes.at[rows], wbuf.at[1, mine], to_y)
    for k in range(1, 4):
        for d in (D_, X_, Y_):
            send_tok(d, k)
    for k in range(4):
        send_tok(O_, k)

    load_cot.wait()
    cot_c.wait_recv()
    cott[...] = cot2[...].astype(F32).T.astype(BF16)

    def grad(d, k):
        own_tok[d, k].wait()
        sib_tok[d, k].wait_recv()
        return jnp.dot(cott[...], tokk[k * 4 + d], preferred_element_type=F32)

    step1x, step1y, step2x, step2y, zc = {}, {}, {}, {}, {}
    slot = {X_: 0, Y_: 1, D_: 2}
    pair, sw = {}, {}

    def spread(d):
        pair[d] = remote(wbuf.at[slot[d], mine], wbuf.at[slot[d], mine], to_pair)
        sw[d, 0] = remote(wbuf.at[slot[d], mine], wbuf.at[slot[d], mine], sib)

    def pass_on(d):
        pair[d].wait_recv()
        sw[d, 1] = remote(wbuf.at[slot[d], theirs], wbuf.at[slot[d], theirs], sib)

    for k in range(4):
        g = grad(D_, k)
        s1x[k, 1] = g[:128].astype(BF16)
        s1y[k, 1] = g[128:].astype(BF16)
        g = grad(X_, k)
        s1x[k, 0] = g[:128].astype(BF16)
        gx[k] = g[128:]
        step1x[k] = remote(s1x.at[k], r1x.at[k], to_x)
        g = grad(Y_, k)
        s1y[k, 0] = g[128:].astype(BF16)
        gy[k] = g[:128]
        step1y[k] = remote(s1y.at[k], r1y.at[k], to_y)
        if k == 1:
            top, bottom = pl.ds(0, 256), pl.ds(256, 256)
            ag[X_].wait_recv()
            ag[D_, 0] = remote(wbuf.at[0, mine, top], wbuf.at[2, mine, top], to_y)
            ag[Y_].wait_recv()
            ag[D_, 1] = remote(wbuf.at[1, mine, bottom], wbuf.at[2, mine, bottom], to_x)
            spread(X_)
            spread(Y_)

    def project(d, load):
        load_tok[d].wait()
        p = scales[pl.ds(pl.multiple_of(dest[d] * 16, 16), 16), :]
        fac = jnp.where(p == 5, 2.0 ** -5, jnp.where(p == 6, 2.0 ** -6, jnp.where(p == 7, 2.0 ** -7, 2.0 ** -8))).astype(F32)
        total = None
        for c in range(4):
            w = load(c).astype(F32)
            w = jnp.concatenate(
                [w[b * 128:(b + 1) * 128] * fac[c * 4 + b:c * 4 + b + 1, :] for b in range(4)], axis=0
            ).astype(BF16)
            part = jnp.dot(tokv[d, :, c * 512:(c + 1) * 512], w, preferred_element_type=F32)
            total = part if total is None else total + part
        return total

    def second(k):
        step1x[k].wait_recv()
        s2y[k] = (gy[k] + r1x[k, 1].astype(F32)).astype(BF16)
        step2y[k] = remote(s2y.at[k], r2y.at[k], to_y)
        step1y[k].wait_recv()
        s2x[k] = (gx[k] + r1y[k, 1].astype(F32)).astype(BF16)
        step2x[k] = remote(s2x.at[k], r2x.at[k], to_x)

    def plane(k):
        step2y[k].wait_recv()
        top = gown[k, :128] + r1x[k, 0].astype(F32) + r2y[k].astype(F32)
        step2x[k].wait_recv()
        bottom = gown[k, 128:] + r1y[k, 0].astype(F32) + r2x[k].astype(F32)
        if k < 3:
            zs[k, :128] = top.astype(BF16)
            zs[k, 128:] = bottom.astype(BF16)
            zc[k] = remote(zs.at[k], zr.at[k], to_z[k])
        else:
            gown[k, :128] = top
            gown[k, 128:] = bottom

    def arrive(d):
        sw[d, 0].wait_recv()
        sw[d, 1].wait_recv()

    for k in range(4):
        gown[k] = grad(O_, k)
    second(0)
    ag[D_, 0].wait_recv()
    ag[D_, 1].wait_recv()
    spread(D_)
    second(1)
    pass_on(X_)
    pass_on(Y_)
    plane(0)
    load_w.wait()
    load_sc.wait()
    acc[...] = project(O_, lambda c: wown[c * 512:(c + 1) * 512])
    second(2)
    plane(1)
    arrive(X_)
    acc[...] += project(X_, lambda c: wbuf[0, c])
    second(3)
    pass_on(D_)
    plane(2)
    arrive(Y_)
    acc[...] += project(Y_, lambda c: wbuf[1, c])
    arrive(D_)
    kv_out[...] = (acc[...] + project(D_, lambda c: wbuf[2, c])).astype(BF16)
    plane(3)
    total = gown[3]
    for k in range(3):
        zc[k].wait_recv()
        total = total + zr[k].astype(F32)
    wg_out[...] = total.T
    for c in sent:
        c.wait_send()


def special(tokens, weight_codes, scale_powers, cotangent):
    T = tokens.shape[0]
    vm = pltpu.VMEM
    n_local, n_remote = 16 + 1 + 4 + 2, 49
    return tuple(pl.pallas_call(
        kernel,
        out_shape=(jax.ShapeDtypeStruct((T, 256), BF16), jax.ShapeDtypeStruct((256, 256), F32)),
        in_specs=[
            pl.BlockSpec(memory_space=pl.ANY), pl.BlockSpec(memory_space=pl.ANY),
            pl.BlockSpec(memory_space=pl.ANY), pl.BlockSpec(memory_space=pl.ANY)],
        out_specs=(pl.BlockSpec(memory_space=vm), pl.BlockSpec(memory_space=vm)),
        scratch_shapes=[
            vm((4, T, 2048), BF16), vm((16, 2 * T, 256), BF16), vm((2 * T, 256), BF16), vm((256, 2 * T), BF16),
            vm((2048, 256), BF16), vm((3, 4, 512, 256), BF16),
            vm((4, 2, 128, 256), BF16), vm((4, 2, 128, 256), BF16),
            vm((4, 2, 128, 256), BF16), vm((4, 2, 128, 256), BF16),
            vm((4, 128, 256), BF16), vm((4, 128, 256), BF16),
            vm((4, 128, 256), BF16), vm((4, 128, 256), BF16),
            vm((4, 256, 256), F32), vm((4, 128, 256), F32), vm((4, 128, 256), F32),
            vm((3, 256, 256), BF16), vm((3, 256, 256), BF16), vm((T, 256), F32),
            vm((64, 256), jnp.int32),
            pltpu.SemaphoreType.DMA((n_local,)),
            pltpu.SemaphoreType.DMA((n_remote,)),
            pltpu.SemaphoreType.DMA((n_remote,)),
        ],
        compiler_params=pltpu.CompilerParams(
            collective_id=0, has_side_effects=True, vmem_limit_bytes=64 * 1024 * 1024 - 65536),
        cost_estimate=pl.CostEstimate(flops=1_700_000_000, bytes_accessed=6_000_000, transcendentals=0),
    )(tokens, weight_codes, scale_powers, cotangent))


def solution(mesh):
    placed = (
        P(("shard", "node", "replica"), None),
        P("shard", None),
        P(),
        P(("shard", "node", "replica"), None),
    )
    small = tuple(mesh.shape[a] for a in ("shard", "node", "replica")) == (4, 4, 2)
    return jax.shard_map(
        special if small else generic,
        mesh=mesh,
        in_specs=placed,
        out_specs=(P(("shard", "node", "replica"), None), P(("shard", "node", "replica"), None)),
        check_vma=False,
    )
```

```python
import functools

import jax
import jax.numpy as jnp
from jax import lax
from jax.experimental import pallas as pl
from jax.experimental.pallas import tpu as pltpu
from jax.sharding import PartitionSpec as P

BLOCK = 128
MESH = pl.DeviceIdType.MESH
OFF = (2, 1, 3, 0)
D_, X_, Y_, O_ = 0, 1, 2, 3
F32, BF16 = jnp.float32, jnp.bfloat16


def generic(tokens, weight_codes, scale_powers, cotangent):
    factors = jnp.repeat(jnp.exp2(-scale_powers.astype(jnp.float32)), BLOCK, axis=0)
    codes = lax.all_gather(weight_codes, "shard", axis=0, tiled=True)
    weight = (codes.astype(jnp.float32) * factors).astype(jnp.bfloat16)
    projected = jnp.dot(tokens, weight, preferred_element_type=jnp.float32)
    keys_values = projected.astype(jnp.bfloat16)
    partial_value = lax.dot_general(
        tokens, cotangent, (((0,), (0,)), ((), ())), preferred_element_type=jnp.float32
    )
    inner = lax.psum_scatter(partial_value, "shard", scatter_dimension=0, tiled=True)
    weight_grad = lax.psum_scatter(inner, ("node", "replica"), scatter_dimension=0, tiled=True)
    return (keys_values, weight_grad)


def kernel(tokens, codes, scales_in, cot, kv_out, wg_out,
           tokv, tokk, cot2, cott, wown, wbuf, s1x, s1y, r1x, r1y,
           s2x, s2y, r2x, r2y, gown, gx, gy, zs, zr, acc, scales, ls, ss, rs):
    s, n, r = lax.axis_index("shard"), lax.axis_index("node"), lax.axis_index("replica")
    xs = s + 1 - 2 * lax.rem(s, 2)
    ys = s + 2 - 4 * lax.div(s, 2)
    dest = (3 - s, xs, ys, s)
    nodes = [lax.rem(n + off, 4) for off in OFF]
    sib, to_x, to_y = {"replica": 1 - r}, {"shard": xs}, {"shard": ys}
    to_z = [{"node": nodes[j]} for j in range(3)]
    T = cot.shape[0]
    par = lax.rem(n, 2)
    mine, theirs = 2 * r + par, 2 * r + 1 - par
    to_pair = {"node": n + 1 - 2 * par}

    nl = [0]
    sent = []

    def local(src, dst):
        c = pltpu.make_async_copy(src, dst, ls.at[nl[0]])
        nl[0] += 1
        c.start()
        return c

    def remote(src, dst, device):
        i = len(sent)
        c = pltpu.make_async_remote_copy(
            src_ref=src, dst_ref=dst, send_sem=ss.at[i], recv_sem=rs.at[i],
            device_id=device, device_id_type=MESH)
        sent.append(c)
        c.start()
        return c

    def columns(d, k, which):
        return pl.ds(pl.multiple_of(((dest[d] * 4 + nodes[k]) * 2 + which) * 256, 256), 256)

    barrier = pltpu.get_barrier_semaphore()
    for peer in [sib, to_x, to_y] + to_z:
        pl.semaphore_signal(barrier, inc=1, device_id=peer, device_id_type=MESH)

    load_cot = local(cot, cot2.at[pl.ds(0, T)])
    load_sc = local(scales_in, scales)
    own_tok = {}
    for k in range(4):
        for d in (D_, X_, Y_):
            own_tok[d, k] = local(tokens.at[:, columns(d, k, r)], tokk.at[k * 4 + d, pl.ds(0, T)])
    pl.semaphore_wait(barrier, 6)

    cot_c = remote(cot, cot2.at[pl.ds(T, T)], sib)
    sib_tok = {}

    def send_tok(d, k):
        sib_tok[d, k] = remote(
            tokens.at[:, columns(d, k, 1 - r)], tokk.at[k * 4 + d, pl.ds(T, T)], sib)

    for d in (D_, X_, Y_):
        send_tok(d, 0)

    half = (pl.ds(0, 256), pl.ds(256, 256))
    ag = {}
    for d, h in ((X_, 0), (Y_, 1), (X_, 1), (Y_, 0)):
        rows = pl.ds(pl.multiple_of(mine * 512 + h * 256, 256), 256)
        ag[d, h] = remote(codes.at[rows], wbuf.at[d - 1, mine, half[h]], to_x if d == X_ else to_y)
    for k in range(1, 4):
        for d in (D_, X_, Y_):
            send_tok(d, k)
    for k in range(4):
        send_tok(O_, k)

    for k in range(4):
        own_tok[O_, k] = local(tokens.at[:, columns(O_, k, r)], tokk.at[k * 4 + O_, pl.ds(0, T)])
    load_w = local(codes, wown)
    load_tok = [None] * 4
    for d in (O_, X_, Y_, D_):
        load_tok[d] = local(
            tokens.at[:, pl.ds(pl.multiple_of(dest[d] * 2048, 2048), 2048)], tokv.at[d])

    load_cot.wait()
    cot_c.wait_recv()
    cott[...] = cot2[...].astype(F32).T.astype(BF16)

    def grad(d, k):
        own_tok[d, k].wait()
        sib_tok[d, k].wait_recv()
        return jnp.dot(cott[...], tokk[k * 4 + d], preferred_element_type=F32)

    step1x, step1y, step2x, step2y, zc = {}, {}, {}, {}, {}
    slot = {X_: 0, Y_: 1, D_: 2}
    pair, sw = {}, {}

    def spread(d, h):
        ag[d, h].wait_recv()
        piece = wbuf.at[slot[d], mine, half[h]]
        if (d, h) == (X_, 0):
            ag[D_, 0] = remote(piece, wbuf.at[2, mine, half[0]], to_y)
        if (d, h) == (Y_, 1):
            ag[D_, 1] = remote(piece, wbuf.at[2, mine, half[1]], to_x)
        pair[d, h] = remote(piece, piece, to_pair)
        sw[d, h, 0] = remote(piece, piece, sib)

    def pass_on(d):
        for h in (0, 1):
            pair[d, h].wait_recv()
            piece = wbuf.at[slot[d], theirs, half[h]]
            sw[d, h, 1] = remote(piece, piece, sib)

    left = []

    def first(k):
        if k >= 2:
            for c in (step1x[k - 2], step1y[k - 2]):
                c.wait_send()
                left.append(c)
        step1x[k] = remote(s1x.at[k], r1x.at[k], to_x)
        step1y[k] = remote(s1y.at[k], r1y.at[k], to_y)

    for k in range(4):
        g = grad(D_, k)
        s1x[k, 1] = g[:128].astype(BF16)
        s1y[k, 1] = g[128:].astype(BF16)
        g = grad(X_, k)
        s1x[k, 0] = g[:128].astype(BF16)
        gx[k] = g[128:]
        g = grad(Y_, k)
        s1y[k, 0] = g[128:].astype(BF16)
        gy[k] = g[:128]
        if k < 2:
            first(k)
        if k == 0:
            spread(X_, 0)
            spread(Y_, 1)
        if k == 1:
            spread(X_, 1)
            spread(Y_, 0)

    def project(d, load):
        load_tok[d].wait()
        p = scales[pl.ds(pl.multiple_of(dest[d] * 16, 16), 16), :]
        fac = jnp.where(p == 5, 2.0 ** -5, jnp.where(p == 6, 2.0 ** -6, jnp.where(p == 7, 2.0 ** -7, 2.0 ** -8))).astype(F32)
        total = None
        for c in range(4):
            w = load(c).astype(F32)
            w = jnp.concatenate(
                [w[b * 128:(b + 1) * 128] * fac[c * 4 + b:c * 4 + b + 1, :] for b in range(4)], axis=0
            ).astype(BF16)
            part = jnp.dot(tokv[d, :, c * 512:(c + 1) * 512], w, preferred_element_type=F32)
            total = part if total is None else total + part
        return total

    def second(k):
        step1x[k].wait_recv()
        s2y[k] = (gy[k] + r1x[k, 1].astype(F32)).astype(BF16)
        step2y[k] = remote(s2y.at[k], r2y.at[k], to_y)
        step1y[k].wait_recv()
        s2x[k] = (gx[k] + r1y[k, 1].astype(F32)).astype(BF16)
        step2x[k] = remote(s2x.at[k], r2x.at[k], to_x)

    def plane(k):
        step2y[k].wait_recv()
        top = gown[k, :128] + r1x[k, 0].astype(F32) + r2y[k].astype(F32)
        step2x[k].wait_recv()
        bottom = gown[k, 128:] + r1y[k, 0].astype(F32) + r2x[k].astype(F32)
        if k < 3:
            zs[k, :128] = top.astype(BF16)
            zs[k, 128:] = bottom.astype(BF16)
            zc[k] = remote(zs.at[k], zr.at[k], to_z[k])
        else:
            gown[k, :128] = top
            gown[k, 128:] = bottom

    def arrive(d):
        for h in (0, 1):
            sw[d, h, 0].wait_recv()
            sw[d, h, 1].wait_recv()

    first(2)
    for k in range(4):
        gown[k] = grad(O_, k)
    spread(D_, 0)
    spread(D_, 1)
    second(0)
    first(3)
    second(1)
    plane(0)
    load_w.wait()
    load_sc.wait()
    acc[...] = project(O_, lambda c: wown[c * 512:(c + 1) * 512])
    second(2)
    plane(1)
    pass_on(X_)
    pass_on(Y_)
    second(3)
    plane(2)
    pass_on(D_)
    arrive(X_)
    acc[...] += project(X_, lambda c: wbuf[0, c])
    arrive(Y_)
    acc[...] += project(Y_, lambda c: wbuf[1, c])
    plane(3)
    arrive(D_)
    kv_out[...] = (acc[...] + project(D_, lambda c: wbuf[2, c])).astype(BF16)
    total = gown[3]
    for k in range(3):
        zc[k].wait_recv()
        total = total + zr[k].astype(F32)
    wg_out[...] = total.T
    for c in sent:
        if all(c is not done for done in left):
            c.wait_send()


def special(tokens, weight_codes, scale_powers, cotangent):
    T = tokens.shape[0]
    vm = pltpu.VMEM
    n_local, n_remote = 16 + 1 + 4 + 2, 60
    return tuple(pl.pallas_call(
        kernel,
        out_shape=(jax.ShapeDtypeStruct((T, 256), BF16), jax.ShapeDtypeStruct((256, 256), F32)),
        in_specs=[
            pl.BlockSpec(memory_space=pl.ANY), pl.BlockSpec(memory_space=pl.ANY),
            pl.BlockSpec(memory_space=pl.ANY), pl.BlockSpec(memory_space=pl.ANY)],
        out_specs=(pl.BlockSpec(memory_space=vm), pl.BlockSpec(memory_space=vm)),
        scratch_shapes=[
            vm((4, T, 2048), BF16), vm((16, 2 * T, 256), BF16), vm((2 * T, 256), BF16), vm((256, 2 * T), BF16),
            vm((2048, 256), BF16), vm((3, 4, 512, 256), BF16),
            vm((4, 2, 128, 256), BF16), vm((4, 2, 128, 256), BF16),
            vm((4, 2, 128, 256), BF16), vm((4, 2, 128, 256), BF16),
            vm((4, 128, 256), BF16), vm((4, 128, 256), BF16),
            vm((4, 128, 256), BF16), vm((4, 128, 256), BF16),
            vm((4, 256, 256), F32), vm((4, 128, 256), F32), vm((4, 128, 256), F32),
            vm((3, 256, 256), BF16), vm((3, 256, 256), BF16), vm((T, 256), F32),
            vm((64, 256), jnp.int32),
            pltpu.SemaphoreType.DMA((n_local,)),
            pltpu.SemaphoreType.DMA((n_remote,)),
            pltpu.SemaphoreType.DMA((n_remote,)),
        ],
        compiler_params=pltpu.CompilerParams(
            collective_id=0, has_side_effects=True, vmem_limit_bytes=64 * 1024 * 1024 - 65536),
        cost_estimate=pl.CostEstimate(flops=1_700_000_000, bytes_accessed=6_000_000, transcendentals=0),
    )(tokens, weight_codes, scale_powers, cotangent))


def solution(mesh):
    placed = (
        P(("shard", "node", "replica"), None),
        P("shard", None),
        P(),
        P(("shard", "node", "replica"), None),
    )
    small = tuple(mesh.shape[a] for a in ("shard", "node", "replica")) == (4, 4, 2)
    return jax.shard_map(
        special if small else generic,
        mesh=mesh,
        in_specs=placed,
        out_specs=(P(("shard", "node", "replica"), None), P(("shard", "node", "replica"), None)),
        check_vma=False,
    )
```
